256 devices in a mesh: grp: 8 (over x, y_hi), seq: 32 (over z, y_lo, core).
Axes of the slice: x: 4, y: 4 (y_hi: 2, y_lo: 2; y = y_hi * 2 + y_lo), z: 8, core: 2. Of those that a mesh axis runs over, the one named last changes fastest.
Arguments:
- query_rows: bfloat16 [49152, 2048], P(('grp', 'seq')), may hold values from -150 to 150
- key_rows: bfloat16 [49152, 2048], P(('grp', 'seq')), may hold values from -5 to 5
- value_rows: bfloat16 [49152, 2048], P(('grp', 'seq')), may hold values from -6 to 6
- cotangent: bfloat16 [49152, 2048], P(('grp', 'seq')), may hold values from -6 to 6
- partner: int32 [8, 32], P('grp'), may hold values from 0 to 31, each once within a row
- anchors: int32 [8], P('grp'), may hold values from 0 to 31
- global_list: int32 [256, 2], P(('grp', 'seq')), may hold values from 0 to 2, as said below
Outputs:
- attended: bfloat16 [49152, 2048], P(('grp', 'seq'))
- grad_queries: bfloat16 [49152, 2048], P(('grp', 'seq'))
- grad_keys: bfloat16 [49152, 2048], P(('grp', 'seq'))
- grad_values: bfloat16 [49152, 2048], P(('grp', 'seq'))
The draws below stay inside these ranges and needn't reach their ends.
Inputs may be any that keep to these rules, and one draw needn't show every extreme that they name: `global_list`: each row lists distinct offsets of 1 to 2 first and zeros after them; offset d in the row of block 32 g + s names the global block of segment (g - d) mod 8.
All inputs are finite; a program needn't handle non-finite values.
Results may differ from the reference program's by a relative error of at most 0.022.
Values may be sent and summed in bfloat16 or wider, within the bound.
A program may use at most 192 MiB of HBM per device.

```python
import jax
import jax.numpy as jnp
from jax import lax

HEAD_DIM = 128
BLOCK = 192
GLOBALS = 2
FEATURES = 2048
BLOCKS = 256
TOKENS = 49152
N_GRP = 8
N_SEQ = 32


def paired_draw(key):
    base_keys = jnp.clip(jax.random.normal(jax.random.fold_in(key, 11), (TOKENS, FEATURES), jnp.float32), -5.0, 5.0)
    base_queries = jnp.clip(jax.random.normal(jax.random.fold_in(key, 12), (TOKENS, FEATURES), jnp.float32), -5.0, 5.0)
    return (base_queries, base_keys)


def draw_query_rows(key, part):
    return paired_draw(key)[0].astype(jnp.bfloat16)


def draw_key_rows(key, part):
    return paired_draw(key)[1].astype(jnp.bfloat16)


def draw_global_list(key, part):
    counted = jax.random.randint(jax.random.fold_in(key, 21), (BLOCKS,), 0, GLOBALS + 1)
    full_row = jax.random.randint(jax.random.fold_in(key, 22), (), 0, BLOCKS)
    counted = jnp.where(jnp.arange(BLOCKS) == full_row, GLOBALS, counted)
    ranking = jax.random.randint(jax.random.fold_in(key, 23), (BLOCKS, GLOBALS), 0, 1 << 20) * GLOBALS + jnp.arange(GLOBALS)[None, :]
    ordering = jnp.argsort(ranking, axis=1).astype(jnp.int32)
    return jnp.where(jnp.arange(GLOBALS)[None, :] < counted[:, None], ordering + 1, 0).astype(jnp.int32)


def touch_ends(result, key, smallest, high):
    longest = result.shape.index(max(result.shape))
    spots = []
    for shift in (0, 1):
        where = [jax.random.randint(jax.random.fold_in(key, axis), (), 0, length) for axis, length in enumerate(result.shape)]
        where[longest] = (where[longest] + shift) % result.shape[longest]
        spots.append(tuple(where))
    return result.at[spots[0]].set(smallest).at[spots[1]].set(high)


def steps_of(own_key, dims, cuts, low, largest):
    gain, own = 1.0, jax.random.fold_in(own_key, 6)
    for dim, blocks in cuts:
        steps = jnp.exp(jax.random.uniform(jax.random.fold_in(own, dim), (blocks,), jnp.float32, low / len(cuts), largest / len(cuts)))
        gain = gain * jnp.repeat(steps, dims[dim] // blocks).reshape([-1 if axis == dim else 1 for axis in range(len(dims))])
    return gain


def noise(own_key, extent, width, reach, pieces=(), kind=jnp.bfloat16):
    loudness = steps_of(own_key, extent, pieces, -0.22, 0.18) if pieces else 1.0
    array = jax.random.normal(own_key, extent, jnp.float32) * width * loudness
    return jnp.minimum(jnp.maximum(array, -reach), reach).astype(kind)


def setup_inputs(seed: int = 0) -> dict:
    key_list = jax.random.split(jax.random.key(seed), 8)
    return {
        "query_rows": draw_query_rows(jax.random.fold_in(key_list[7], 71), 0),
        "key_rows": draw_key_rows(jax.random.fold_in(key_list[7], 71), 0),
        "value_rows": noise(key_list[2], (TOKENS, FEATURES), 1.0, 6.0, ((0, 256),)),
        "cotangent": noise(key_list[3], (TOKENS, FEATURES), 1.0, 6.0, ((0, 256),)),
        "partner": jax.vmap(lambda own: jax.random.permutation(own, N_SEQ))(jax.random.split(key_list[4], N_GRP)).reshape((N_GRP, N_SEQ)).astype(jnp.int32),
        "anchors": touch_ends(jax.random.randint(key_list[5], (N_GRP,), 0, N_SEQ), jax.random.fold_in(key_list[5], 1), 0, N_SEQ - 1).astype(jnp.int32),
        "global_list": draw_global_list(jax.random.fold_in(key_list[7], 71), 0),
    }


def rounded(values_in):
    return lax.optimization_barrier(values_in.astype(jnp.bfloat16)).astype(jnp.float32)


def attend_block(query_block, key_set, value_set, live_mask, grad_block):
    heads_here = query_block.shape[1] // HEAD_DIM
    scaling = HEAD_DIM ** -0.5
    query_heads = query_block.astype(jnp.float32).reshape(-1, heads_here, HEAD_DIM)
    key_heads = key_set.astype(jnp.float32).reshape(-1, heads_here, HEAD_DIM)
    value_heads = value_set.astype(jnp.float32).reshape(-1, heads_here, HEAD_DIM)
    grad_heads = grad_block.astype(jnp.float32).reshape(-1, heads_here, HEAD_DIM)
    scores = jnp.einsum("qhd,khd->hqk", query_heads, key_heads) * scaling
    scores = jnp.where(live_mask[None, None, :], scores, -jnp.inf)
    row_top = jnp.max(scores, axis=-1, keepdims=True)
    lifted = jnp.exp(scores - row_top)
    probs = lifted / jnp.sum(lifted, axis=-1, keepdims=True)
    weights = rounded(probs)
    width_all = query_block.shape[1]
    attended = jnp.einsum("hqk,khd->qhd", weights, value_heads).reshape(-1, width_all).astype(jnp.bfloat16)
    dprob = jnp.einsum("qhd,khd->hqk", grad_heads, value_heads)
    delta = jnp.sum(probs * dprob, axis=-1, keepdims=True)
    dscore = rounded(probs * (dprob - delta))
    grad_query = (jnp.einsum("hqk,khd->qhd", dscore, key_heads) * scaling).reshape(-1, width_all).astype(jnp.bfloat16)
    key_terms = (jnp.einsum("hqk,qhd->khd", dscore, query_heads) * scaling).reshape(-1, width_all)
    value_terms = jnp.einsum("hqk,qhd->khd", weights, grad_heads).reshape(-1, width_all)
    return attended, grad_query, key_terms, value_terms


def reference(query_rows, key_rows, value_rows, cotangent, partner, anchors, global_list):
    blocks_all = N_GRP * N_SEQ
    width_all = query_rows.shape[1]
    query_blocks = query_rows.reshape(blocks_all, BLOCK, width_all)
    key_blocks = key_rows.reshape(blocks_all, BLOCK, width_all)
    value_blocks = value_rows.reshape(blocks_all, BLOCK, width_all)
    grad_blocks = cotangent.reshape(blocks_all, BLOCK, width_all)

    def step(carry, position):
        key_acc, value_acc = carry
        group = position // N_SEQ
        seat = position % N_SEQ
        mate = group * N_SEQ + partner[group, seat]
        sources = [position, mate]
        listed = []
        for offset in range(1, GLOBALS + 1):
            other = (group - offset) % N_GRP
            sources.append(other * N_SEQ + anchors[other])
            listed.append(jnp.any(global_list[position] == offset))
        key_set = jnp.concatenate([key_blocks[source] for source in sources], 0)
        value_set = jnp.concatenate([value_blocks[source] for source in sources], 0)
        live_mask = jnp.concatenate([jnp.ones((2 * BLOCK,), bool)] + [jnp.broadcast_to(flag, (BLOCK,)) for flag in listed])
        attended, grad_query, key_terms, value_terms = attend_block(query_blocks[position], key_set, value_set, live_mask, grad_blocks[position])
        key_terms = key_terms.reshape(2 + GLOBALS, BLOCK, width_all)
        value_terms = value_terms.reshape(2 + GLOBALS, BLOCK, width_all)
        key_acc = key_acc.at[position].add(key_terms[0])
        value_acc = value_acc.at[position].add(value_terms[0])
        for number in range(1, 2 + GLOBALS):
            key_acc = key_acc.at[sources[number]].add(rounded(key_terms[number]))
            value_acc = value_acc.at[sources[number]].add(rounded(value_terms[number]))
        return (key_acc, value_acc), (attended, grad_query)

    zeros_acc = jnp.zeros((blocks_all, BLOCK, width_all), jnp.float32)
    (key_acc, value_acc), (attended, grad_query) = lax.scan(step, (zeros_acc, zeros_acc), jnp.arange(blocks_all, dtype=jnp.int32))
    total_rows = blocks_all * BLOCK
    return (attended.reshape(total_rows, width_all), grad_query.reshape(total_rows, width_all), key_acc.reshape(total_rows, width_all).astype(jnp.bfloat16), value_acc.reshape(total_rows, width_all).astype(jnp.bfloat16))
```

```python
import functools

import jax
import jax.numpy as jnp
from jax import lax
from jax.experimental import pallas as pl
from jax.experimental.pallas import tpu as pltpu
from jax.sharding import PartitionSpec as P

HEAD_DIM = 128
GLOBALS = 2
MESH = pl.DeviceIdType.MESH
LOG2E = 1.4426950408889634
F32, BF16 = jnp.float32, jnp.bfloat16


def matmul(a, b, ca, cb):
    return lax.dot_general(a, b, (((ca,), (cb,)), ((), ())), preferred_element_type=F32)


def kernel(
    groups, chips, rows,
    q_ref, k_ref, v_ref, g_ref, partner_ref, anchor_ref, list_ref,
    o_ref, dq_ref, dk_ref, dv_ref,
    kb, vb, qb, gb, ob, dqb, okt, ovt, pkt, pvt, dkb, dvb,
    kc, vc, live, bias, anchor_kv, gterm, gsend, grecv, gown, gother,
    in_send, in_recv, live_send, live_recv, local, swap_send, swap_recv,
    anchor_send, anchor_recv, out_send, out_recv, term_send, term_recv,
    gterm_send, gterm_recv, gswap_send, gswap_recv,
):
    seat, grp = lax.axis_index("seq"), lax.axis_index("grp")
    chip, core = lax.div(seat, 2), lax.rem(seat, 2)
    half = chips // 2
    scale = HEAD_DIM**-0.5
    mate = {"seq": chip * 2 + (1 - core)}

    def ring(n):
        return half + (2 * lax.rem(n, 2) - 1) * lax.div(n + 1, 2)

    def ahead(n):
        return lax.rem(chip + ring(n), chips)

    def behind(n):
        return lax.rem(chip - ring(n) + chips, chips)

    def columns(head):
        return pl.ds(pl.multiple_of(head * HEAD_DIM, HEAD_DIM), HEAD_DIM)

    def peer(other):
        return {"seq": other * 2 + core}

    def segment(offset):
        return {"grp": lax.rem(grp + offset + groups, groups)}

    def slot(block):
        return lax.div(block, 2) + chips * lax.rem(lax.rem(block, 2) + core, 2)

    def remote(src, dst, send, recv, device):
        return pltpu.make_async_remote_copy(
            src_ref=src, dst_ref=dst, send_sem=send, recv_sem=recv, device_id=device, device_id_type=MESH
        )

    inputs = ((k_ref, kb), (v_ref, vb), (q_ref, qb), (g_ref, gb))

    def bring(a, n):
        src, dst = inputs[a]
        to = ahead(n)
        return remote(src.at[:, columns(to)], dst.at[chip], in_send.at[a, n], in_recv.at[a, n], peer(to))

    def brought(a, n):
        src, dst = inputs[a]
        return remote(src.at[:, columns(chip)], dst.at[behind(n)], in_send.at[a, n], in_recv.at[a, n], peer(behind(n)))

    def own_in(a):
        src, dst = inputs[a]
        return pltpu.make_async_copy(src.at[:, columns(chip)], dst.at[chip], local.at[a])

    def show(n):
        return remote(live, bias.at[chip], live_send.at[n], live_recv.at[n], peer(ahead(n)))

    def shown(n):
        return remote(live, bias.at[behind(n)], live_send.at[n], live_recv.at[n], peer(behind(n)))

    outputs = ((ob, o_ref), (dqb, dq_ref), (dkb, dk_ref), (dvb, dv_ref))

    def give(a, n):
        src, dst = outputs[a]
        to = behind(n)
        return remote(src.at[to], dst.at[:, columns(chip)], out_send.at[a, n], out_recv.at[a, n], peer(to))

    def given(a, n):
        src, dst = outputs[a]
        come = ahead(n)
        return remote(src.at[chip], dst.at[:, columns(come)], out_send.at[a, n], out_recv.at[a, n], peer(come))

    def own_out(a):
        src, dst = outputs[a]
        return pltpu.make_async_copy(src.at[chip], dst.at[:, columns(chip)], local.at[4 + a])

    def swap(a, s):
        buf = (kb, vb)[a]
        return remote(buf.at[s], buf.at[chips + s], swap_send.at[a, s], swap_recv.at[a, s], mate)

    def swap_terms(a, s):
        buf = (pkt, pvt)[a]
        return remote(buf.at[s], buf.at[chips + s], term_send.at[a, s], term_recv.at[a, s], mate)

    def anchor_out(a, d):
        dst = (kc, vc)[a]
        return remote(
            anchor_kv.at[a], dst.at[pl.ds((1 + d) * rows, rows)], anchor_send.at[a, d - 1], anchor_recv.at[a, d - 1],
            segment(d),
        )

    def gterm_out(d):
        return remote(gsend.at[d - 1], grecv.at[d - 1], gterm_send.at[d - 1], gterm_recv.at[d - 1], segment(-d))

    def gswap():
        return remote(gown, gother, gswap_send.at[0], gswap_recv.at[0], mate)

    def loop(count, body):
        def step(n, carry):
            body(n)
            return carry

        lax.fori_loop(0, count, step, 0)

    listed = [
        jnp.where((list_ref[0, 0] == d) | (list_ref[0, 1] == d), 0.0, -jnp.inf).astype(F32) for d in (1, 2)
    ]
    lane = lax.broadcasted_iota(jnp.int32, live.shape, 1)
    live[...] = jnp.where(lane < rows, listed[0], listed[1])

    barrier = pltpu.get_barrier_semaphore()

    def greet(n):
        pl.semaphore_signal(barrier, inc=1, device_id=peer(ahead(n)), device_id_type=MESH)

    pl.semaphore_signal(barrier, inc=1, device_id=mate, device_id_type=MESH)
    loop(chips - 1, greet)
    for d in (1, 2, -1, -2):
        pl.semaphore_signal(barrier, inc=1, device_id=segment(d), device_id_type=MESH)
    pl.semaphore_wait(barrier, chips + 4)

    def send_kv(n):
        bring(0, n).start()
        bring(1, n).start()

    def send_qg(n):
        bring(2, n).start()
        bring(3, n).start()
        show(n).start()

    for a in range(4):
        own_in(a).start()
    loop(chips - 1, send_kv)
    loop(chips - 1, send_qg)
    bias[chip] = live[...]
    gterm[...] = jnp.zeros_like(gterm)

    for a in range(4):
        own_in(a).wait()
    for a in range(2):
        swap(a, chip).start()

    def pass_on(n):
        for a in range(2):
            brought(a, n).wait_recv()
            swap(a, behind(n)).start()

    loop(chips - 1, pass_on)

    def swapped(s):
        for a in range(2):
            swap(a, s).wait_recv()

    loop(chips, swapped)

    anchor = anchor_ref[0]
    anchor_kv[0] = kb[slot(anchor)]
    anchor_kv[1] = vb[slot(anchor)]
    for d in (1, 2):
        for a in range(2):
            anchor_out(a, d).start()
    for d in (1, 2):
        for a in range(2):
            anchor_out(a, d).wait_recv()

    def attend(i):
        n = lax.rem(i + chips - 1, chips)
        at = behind(n)

        @pl.when(i > 0)
        def _():
            brought(2, n).wait_recv()
            brought(3, n).wait_recv()
            shown(n).wait_recv()

        partner = slot(partner_ref[0, 2 * at + core])
        kc[pl.ds(0, rows)] = kb[at]
        kc[pl.ds(rows, rows)] = kb[partner]
        vc[pl.ds(0, rows)] = vb[at]
        vc[pl.ds(rows, rows)] = vb[partner]
        query, grad, keys, values = qb[at], gb[at], kc[...], vc[...]
        scores = matmul(query, keys, 1, 1)
        both, far = scores[:, : 2 * rows], scores[:, 2 * rows :] + bias[at][:1]
        scores = jnp.concatenate([both, far], 1)
        top = jnp.max(scores, axis=1, keepdims=True)
        lifted = jnp.exp2((scores - top) * (scale * LOG2E))
        probs = lifted * (1.0 / jnp.sum(lifted, axis=1, keepdims=True))
        weights = probs.astype(BF16)
        ob[at] = matmul(weights, values, 1, 0).astype(BF16)
        dprob = matmul(grad, values, 1, 1)
        delta = jnp.sum(probs * dprob, axis=1, keepdims=True)
        dscore = (probs * (dprob - delta)).astype(BF16)
        dqb[at] = (matmul(dscore, keys, 1, 0) * scale).astype(BF16)
        key_terms = matmul(dscore, query, 0, 0) * scale
        okt[at] = key_terms[:rows]
        pkt[at] = key_terms[rows : 2 * rows].astype(BF16)
        gterm[0] += key_terms[2 * rows :]
        value_terms = matmul(weights, grad, 0, 0)
        ovt[at] = value_terms[:rows]
        pvt[at] = value_terms[rows : 2 * rows].astype(BF16)
        gterm[1] += value_terms[2 * rows :]

        @pl.when(i > 0)
        def _():
            give(0, n).start()
            give(1, n).start()

        @pl.when(i == 0)
        def _():
            own_out(0).start()
            own_out(1).start()

        swap_terms(0, at).start()
        swap_terms(1, at).start()

    loop(chips, attend)

    for d in (1, 2):
        for a in range(2):
            gsend[d - 1, a] = gterm[a, (d - 1) * rows : d * rows].astype(BF16)
        gterm_out(d).start()
    for d in (1, 2):
        gterm_out(d).wait_recv()
    gown[...] = (grecv[0].astype(F32) + grecv[1].astype(F32)).astype(BF16)
    gswap().start()

    def terms_swapped(s):
        for a in range(2):
            swap_terms(a, s).wait_recv()

    loop(chips, terms_swapped)
    gswap().wait_recv()

    def finish(i):
        n = lax.rem(i + chips - 1, chips)
        at = behind(n)
        block = 2 * at + core
        source = jnp.int32(0)
        for s in range(2 * chips):
            source = jnp.where(partner_ref[0, s] == block, s, source)
        source = slot(source)
        here = jnp.where(anchor == block, 1.0, 0.0).astype(F32)
        for a, (own, far, out) in enumerate(((okt, pkt, dkb), (ovt, pvt, dvb))):
            back = grecv[0, a].astype(F32) + grecv[1, a].astype(F32) + gother[a].astype(F32)
            out[at] = (own[at] + far[source].astype(F32) + here * back).astype(BF16)

        @pl.when(i > 0)
        def _():
            give(2, n).start()
            give(3, n).start()

        @pl.when(i == 0)
        def _():
            own_out(2).start()
            own_out(3).start()

    loop(chips, finish)

    def sent(n):
        for a in range(4):
            bring(a, n).wait_send()
        show(n).wait_send()

    loop(chips - 1, sent)

    def swaps_sent(s):
        for a in range(2):
            swap(a, s).wait_send()
            swap_terms(a, s).wait_send()

    loop(chips, swaps_sent)
    for d in (1, 2):
        for a in range(2):
            anchor_out(a, d).wait_send()
        gterm_out(d).wait_send()
    gswap().wait_send()
    for a in range(4):
        own_out(a).wait()

    def done(n):
        for a in range(4):
            give(a, n).wait_send()
            given(a, n).wait_recv()

    loop(chips - 1, done)


def on_device(groups, seats, query_rows, key_rows, value_rows, cotangent, partner, anchors, global_list):
    rows, width = query_rows.shape
    chips = seats // 2
    hbm, anywhere = pl.BlockSpec(memory_space=pltpu.HBM), pl.BlockSpec(memory_space=pl.ANY)
    smem = pl.BlockSpec(memory_space=pltpu.SMEM)
    vmem, dma = pltpu.VMEM, pltpu.SemaphoreType.DMA
    piece = (rows, HEAD_DIM)
    wide = (GLOBALS * rows, HEAD_DIM)
    return pl.pallas_call(
        functools.partial(kernel, groups, chips, rows),
        out_shape=[jax.ShapeDtypeStruct((rows, width), BF16)] * 4,
        in_specs=[hbm] * 4 + [smem] * 3,
        out_specs=[anywhere] * 4,
        scratch_shapes=[
            vmem((2 * chips, *piece), BF16),
            vmem((2 * chips, *piece), BF16),
            vmem((chips, *piece), BF16),
            vmem((chips, *piece), BF16),
            vmem((chips, *piece), BF16),
            vmem((chips, *piece), BF16),
            vmem((chips, *piece), F32),
            vmem((chips, *piece), F32),
            vmem((2 * chips, *piece), BF16),
            vmem((2 * chips, *piece), BF16),
            vmem((chips, *piece), BF16),
            vmem((chips, *piece), BF16),
            vmem(((2 + GLOBALS) * rows, HEAD_DIM), BF16),
            vmem(((2 + GLOBALS) * rows, HEAD_DIM), BF16),
            vmem((8, GLOBALS * rows), F32),
            vmem((chips, 8, GLOBALS * rows), F32),
            vmem((2, *piece), BF16),
            vmem((2, *wide), F32),
            vmem((2, 2, *piece), BF16),
            vmem((2, 2, *piece), BF16),
            vmem((2, *piece), BF16),
            vmem((2, *piece), BF16),
            dma((4, chips)), dma((4, chips)),
            dma((chips,)), dma((chips,)),
            dma((8,)),
            dma((2, chips)), dma((2, chips)),
            dma((2, 2)), dma((2, 2)),
            dma((4, chips)), dma((4, chips)),
            dma((2, chips)), dma((2, chips)),
            dma((2,)), dma((2,)),
            dma((1,)), dma((1,)),
        ],
        compiler_params=pltpu.CompilerParams(
            collective_id=0, has_side_effects=True, vmem_limit_bytes=48 * 2**20
        ),
        cost_estimate=pl.CostEstimate(flops=3_700_000_000, bytes_accessed=6_300_000, transcendentals=2_400_000),
    )(query_rows, key_rows, value_rows, cotangent, partner, anchors, global_list)


def solution(mesh):
    rows = P(("grp", "seq"), None)
    return jax.shard_map(
        functools.partial(on_device, mesh.shape["grp"], mesh.shape["seq"]),
        mesh=mesh,
        in_specs=(rows, rows, rows, rows, P("grp", None), P("grp"), rows),
        out_specs=(rows, rows, rows, rows),
        check_vma=False,
    )
```

```python
import functools

import jax
import jax.numpy as jnp
from jax import lax
from jax.experimental import pallas as pl
from jax.experimental.pallas import tpu as pltpu
from jax.sharding import PartitionSpec as P

HEAD_DIM = 128
GLOBALS = 2
MESH = pl.DeviceIdType.MESH
LOG2E = 1.4426950408889634
VMEM_LIMIT = 62 * 2**20
PARTS = 2
F32, BF16 = jnp.float32, jnp.bfloat16


def matmul(a, b, ca, cb):
    return lax.dot_general(a, b, (((ca,), (cb,)), ((), ())), preferred_element_type=F32)


def kernel(
    groups, chips, rows,
    q_ref, k_ref, v_ref, g_ref, partner_hbm, anchor_hbm, list_hbm,
    o_ref, dq_ref, dk_ref, dv_ref,
    partner_ref, anchor_ref, list_ref,
    kv, qg, odq, dkv, own_terms, terms, key_set, live, bias, anchor_kv, gterm, gsend, grecv, gown, gother,
    small, local, in_send, kv_recv, qg_recv, live_sem, swap_sem, term_sem, anchor_sem, out_send, out_recv,
    gterm_sem, gswap_sem,
):
    seat, grp = lax.axis_index("seq"), lax.axis_index("grp")
    chip, core = lax.div(seat, 2), lax.rem(seat, 2)
    half, others = chips // 2, chips - 1
    scale = HEAD_DIM**-0.5
    mate = {"seq": chip * 2 + (1 - core)}

    def ring(n):
        return half + (2 * lax.rem(n, 2) - 1) * lax.div(n + 1, 2)

    def ahead(n):
        return lax.rem(chip + ring(n), chips)

    def behind(n):
        return lax.rem(chip - ring(n) + chips, chips)

    def columns(head):
        return pl.ds(pl.multiple_of(head * HEAD_DIM, HEAD_DIM), HEAD_DIM)

    def peer(other):
        return {"seq": other * 2 + core}

    def segment(offset):
        return {"grp": lax.rem(grp + offset + groups, groups)}

    def slot(block):
        return lax.div(block, 2) + chips * lax.rem(lax.rem(block, 2) + core, 2)

    def remote(src, dst, send, recv, device):
        return pltpu.make_async_remote_copy(
            src_ref=src, dst_ref=dst, send_sem=send, recv_sem=recv, device_id=device, device_id_type=MESH
        )

    def take(ref, sem):
        pltpu.make_async_copy(ref, ref, sem).wait()

    def bring(refs, buf, send, recv, n):
        to = ahead(n)
        for a in range(2):
            remote(refs[a].at[:, columns(to)], buf.at[chip, a], send, recv.at[n], peer(to)).start()

    def give(buf, refs, sems, n):
        to = behind(n)
        for a in range(2):
            remote(buf.at[to, a], refs[a].at[:, columns(chip)], out_send.at[sems], out_recv.at[sems], peer(to)).start()

    def own_in(refs, buf, sem):
        return [pltpu.make_async_copy(refs[a].at[:, columns(chip)], buf.at[chip, a], local.at[sem + a]) for a in range(2)]

    def own_out(buf, refs, sem):
        return [pltpu.make_async_copy(buf.at[chip, a], refs[a].at[:, columns(chip)], local.at[sem + a]) for a in range(2)]

    def show(n):
        return remote(live, bias.at[chip], live_sem.at[0], live_sem.at[1], peer(ahead(n)))

    def swap(buf, sems, s):
        return remote(buf.at[s], buf.at[chips + s], sems.at[0], sems.at[1], mate)

    def anchor_out(a, d):
        dst = key_set.at[a, pl.ds((1 + d) * rows, rows)]
        return remote(anchor_kv.at[a], dst, anchor_sem.at[0], anchor_sem.at[1], segment(d))

    def gterm_out(d):
        return remote(gsend.at[d - 1], grecv.at[d - 1], gterm_sem.at[0], gterm_sem.at[1], segment(-d))

    def gswap():
        return remote(gown, gother, gswap_sem.at[0], gswap_sem.at[1], mate)

    def loop(count, body):
        def step(n, carry):
            body(n)
            return carry

        lax.fori_loop(0, count, step, 0)

    scalars = [
        pltpu.make_async_copy(src, dst, small.at[a])
        for a, (src, dst) in enumerate(((partner_hbm, partner_ref), (anchor_hbm, anchor_ref), (list_hbm, list_ref)))
    ]
    for copy in scalars:
        copy.start()
    inputs_kv, inputs_qg = (k_ref, v_ref), (q_ref, g_ref)
    for copy in own_in(inputs_kv, kv, 0) + own_in(inputs_qg, qg, 2):
        copy.start()

    barrier = pltpu.get_barrier_semaphore()

    def greet(n):
        pl.semaphore_signal(barrier, inc=1, device_id=peer(ahead(n)), device_id_type=MESH)

    pl.semaphore_signal(barrier, inc=1, device_id=mate, device_id_type=MESH)
    loop(others, greet)
    for d in (1, 2, -1, -2):
        pl.semaphore_signal(barrier, inc=1, device_id=segment(d), device_id_type=MESH)
    for copy in scalars:
        copy.wait()
    for d in (1, 2):
        listed = jnp.where((list_ref[0, 0] == d) | (list_ref[0, 1] == d), 0.0, -jnp.inf).astype(F32)
        live[d - 1 : d] = jnp.full((1, HEAD_DIM), listed)
    pl.semaphore_wait(barrier, chips + 4)

    loop(others, lambda n: show(n).start())
    loop(others, lambda n: bring(inputs_kv, kv, in_send.at[0], kv_recv, n))
    loop(others, lambda n: bring(inputs_qg, qg, in_send.at[1], qg_recv, n))
    bias[chip] = live[...]
    gterm[...] = jnp.zeros_like(gterm)

    for copy in own_in(inputs_kv, kv, 0):
        copy.wait()
    swap(kv, swap_sem, chip).start()

    def pass_on(n):
        take(kv.at[behind(n)], kv_recv.at[n])
        swap(kv, swap_sem, behind(n)).start()

    loop(others, pass_on)
    take(kv.at[pl.ds(chips, chips)], swap_sem.at[1])

    anchor = anchor_ref[0]
    anchor_kv[...] = kv[slot(anchor)]
    for d in (1, 2):
        for a in range(2):
            anchor_out(a, d).start()
    for copy in own_in(inputs_qg, qg, 2):
        copy.wait()
    take(bias.at[pl.ds(0, others)], live_sem.at[1])
    take(key_set.at[:, pl.ds(2 * rows, GLOBALS * rows)], anchor_sem.at[1])

    def attend(i):
        n = lax.rem(i + others, chips)
        at = behind(n)

        @pl.when(i > 0)
        def _():
            take(qg.at[at], qg_recv.at[n])

        partner = slot(partner_ref[0, 2 * at + core])
        key_set[:, pl.ds(0, rows)] = kv[at]
        key_set[:, pl.ds(rows, rows)] = kv[partner]
        query, grad, keys, values = qg[at, 0], qg[at, 1], key_set[0], key_set[1]
        scores = matmul(query, keys, 1, 1)
        lane = lax.broadcasted_iota(jnp.int32, (1, HEAD_DIM), 1)
        first, second = bias[at][:1], bias[at][1:]
        offsets = [
            first if at_lane + HEAD_DIM <= rows else second if at_lane >= rows else jnp.where(lane < rows - at_lane, first, second)
            for at_lane in range(0, GLOBALS * rows, HEAD_DIM)
        ]
        offset = jnp.concatenate(offsets, 1)[:, : GLOBALS * rows]
        scores = jnp.concatenate([scores[:, : 2 * rows], scores[:, 2 * rows :] + offset], 1)
        top = jnp.max(scores, axis=1, keepdims=True)
        lifted = jnp.exp2((scores - top) * (scale * LOG2E))
        probs = lifted * (1.0 / jnp.sum(lifted, axis=1, keepdims=True))
        weights = probs.astype(BF16)
        odq[at, 0] = matmul(weights, values, 1, 0).astype(BF16)
        dprob = matmul(grad, values, 1, 1)
        delta = jnp.sum(probs * dprob, axis=1, keepdims=True)
        dscore = (probs * (dprob - delta)).astype(BF16)
        odq[at, 1] = (matmul(dscore, keys, 1, 0) * scale).astype(BF16)
        for a, term in enumerate((matmul(dscore, query, 0, 0) * scale, matmul(weights, grad, 0, 0))):
            own_terms[at, a] = term[:rows]
            terms[at, a] = term[rows : 2 * rows].astype(BF16)
            gterm[a] += term[2 * rows :]

        @pl.when(i > 0)
        def _():
            give(odq, (o_ref, dq_ref), 0, n)

        @pl.when(i == 0)
        def _():
            for copy in own_out(odq, (o_ref, dq_ref), 0):
                copy.start()

        swap(terms, term_sem, at).start()

    loop(chips, attend)

    for d in (1, 2):
        for a in range(2):
            gsend[d - 1, a] = gterm[a, (d - 1) * rows : d * rows].astype(BF16)
        gterm_out(d).start()
    take(grecv, gterm_sem.at[1])
    gown[...] = (grecv[0].astype(F32) + grecv[1].astype(F32)).astype(BF16)
    gswap().start()
    take(terms.at[pl.ds(chips, chips)], term_sem.at[1])
    take(gother, gswap_sem.at[1])

    def finish(i):
        n = lax.rem(i + others, chips)
        at = behind(n)
        block = 2 * at + core
        source = jnp.int32(0)
        for s in range(2 * chips):
            source = jnp.where(partner_ref[0, s] == block, s, source)
        source = slot(source)
        here = jnp.where(anchor == block, 1.0, 0.0).astype(F32)
        back = grecv[0].astype(F32) + grecv[1].astype(F32) + gother[...].astype(F32)
        dkv[at] = (own_terms[at] + terms[source].astype(F32) + here * back).astype(BF16)

        @pl.when(i > 0)
        def _():
            give(dkv, (dk_ref, dv_ref), 1, n)

        @pl.when(i == 0)
        def _():
            for copy in own_out(dkv, (dk_ref, dv_ref), 2):
                copy.start()

    loop(chips, finish)

    for a, buf in enumerate((kv, qg)):
        take(buf.at[pl.ds(0, others)], in_send.at[a])
    take(bias.at[pl.ds(0, others)], live_sem.at[0])
    take(kv.at[pl.ds(0, chips)], swap_sem.at[0])
    take(terms.at[pl.ds(0, chips)], term_sem.at[0])
    take(key_set.at[:, pl.ds(2 * rows, GLOBALS * rows)], anchor_sem.at[0])
    take(gsend, gterm_sem.at[0])
    take(gown, gswap_sem.at[0])
    for copy in own_out(odq, (o_ref, dq_ref), 0) + own_out(dkv, (dk_ref, dv_ref), 2):
        copy.wait()
    for sems in range(2):
        take(odq.at[pl.ds(0, others)], out_send.at[sems])
        take(odq.at[pl.ds(0, others)], out_recv.at[sems])


def write_out(parts, *refs):
    held, arrive, leave = refs[8:]
    height = held.shape[1] // parts

    def each(make):
        return [make(a, pl.ds(p * height, height), a * parts + p) for p in range(parts) for a in range(4)]

    arriving = each(lambda a, at, n: pltpu.make_async_copy(refs[a].at[at], held.at[a, at], arrive.at[n]))
    leaving = each(lambda a, at, n: pltpu.make_async_copy(held.at[a, at], refs[4 + a].at[at], leave.at[n]))
    for copy in arriving:
        copy.start()
    for come, go in zip(arriving, leaving, strict=True):
        come.wait()
        go.start()
    for copy in leaving:
        copy.wait()


def on_device(groups, seats, query_rows, key_rows, value_rows, cotangent, partner, anchors, global_list):
    rows, width = query_rows.shape
    chips = seats // 2
    anywhere = pl.BlockSpec(memory_space=pl.ANY)
    vmem, smem, dma = pltpu.VMEM, pltpu.SMEM, pltpu.SemaphoreType.DMA
    piece = (rows, HEAD_DIM)
    pair = (2, *piece)
    results = pl.pallas_call(
        functools.partial(kernel, groups, chips, rows),
        out_shape=[jax.ShapeDtypeStruct((rows, width), BF16)] * 4,
        in_specs=[anywhere] * 7,
        out_specs=[anywhere] * 4,
        scratch_shapes=[
            smem(partner.shape, jnp.int32),
            smem(anchors.shape, jnp.int32),
            smem(global_list.shape, jnp.int32),
            vmem((2 * chips, *pair), BF16),
            vmem((chips, *pair), BF16),
            vmem((chips, *pair), BF16),
            vmem((chips, *pair), BF16),
            vmem((chips, *pair), F32),
            vmem((2 * chips, *pair), BF16),
            vmem((2, (2 + GLOBALS) * rows, HEAD_DIM), BF16),
            vmem((2, HEAD_DIM), F32),
            vmem((chips, 2, HEAD_DIM), F32),
            vmem(pair, BF16),
            vmem((2, GLOBALS * rows, HEAD_DIM), F32),
            vmem((GLOBALS, *pair), BF16),
            vmem((GLOBALS, *pair), BF16),
            vmem(pair, BF16),
            vmem(pair, BF16),
            dma((3,)),
            dma((4,)),
            dma((2,)),
            dma((chips - 1,)),
            dma((chips - 1,)),
            dma((2,)),
            dma((2,)),
            dma((2,)),
            dma((2,)),
            dma((2,)),
            dma((2,)),
            dma((2,)),
            dma((2,)),
        ],
        compiler_params=pltpu.CompilerParams(collective_id=0, has_side_effects=True, vmem_limit_bytes=VMEM_LIMIT),
        cost_estimate=pl.CostEstimate(flops=3_700_000_000, bytes_accessed=6_300_000, transcendentals=2_400_000),
    )(query_rows, key_rows, value_rows, cotangent, partner, anchors, global_list)
    return pl.pallas_call(
        functools.partial(write_out, PARTS),
        out_shape=[jax.ShapeDtypeStruct((rows, width), BF16)] * 4,
        in_specs=[anywhere] * 4,
        out_specs=[anywhere] * 4,
        scratch_shapes=[vmem((4, rows, width), BF16), dma((4 * PARTS,)), dma((4 * PARTS,))],
    )(*results)


def solution(mesh):
    rows = P(("grp", "seq"), None)
    return jax.shard_map(
        functools.partial(on_device, mesh.shape["grp"], mesh.shape["seq"]),
        mesh=mesh,
        in_specs=(rows, rows, rows, rows, P("grp", None), P("grp"), rows),
        out_specs=(rows, rows, rows, rows),
        check_vma=False,
    )
```

```python
import functools

import jax
import jax.numpy as jnp
from jax import lax
from jax.experimental import pallas as pl
from jax.experimental.pallas import tpu as pltpu
from jax.sharding import PartitionSpec as P

HEAD_DIM = 128
GLOBALS = 2
MESH = pl.DeviceIdType.MESH
LOG2E = 1.4426950408889634
VMEM_LIMIT = 62 * 2**20
PARTS = 2
F32, BF16 = jnp.float32, jnp.bfloat16


def matmul(a, b, ca, cb):
    return lax.dot_general(a, b, (((ca,), (cb,)), ((), ())), preferred_element_type=F32)


def kernel(
    groups, chips, rows,
    q_ref, k_ref, v_ref, g_ref, partner_hbm, anchor_hbm, list_hbm,
    o_ref, dq_ref, dk_ref, dv_ref,
    partner_ref, anchor_ref, list_ref,
    kv, qg, odq, dkv, own_terms, terms, key_set, live, bias, anchor_kv, gterm, gsend, grecv, gown, gother,
    small, local, in_send, kv_recv, qg_recv, live_sem, swap_sem, term_sem, anchor_sem, out_send, out_recv,
    gterm_sem, gswap_sem,
):
    seat, grp = lax.axis_index("seq"), lax.axis_index("grp")
    chip, core = lax.div(seat, 2), lax.rem(seat, 2)
    half, others = chips // 2, chips - 1
    scale = HEAD_DIM**-0.5
    mate = {"seq": chip * 2 + (1 - core)}

    def ring(n):
        return half + (2 * lax.rem(n, 2) - 1) * lax.div(n + 1, 2)

    def ahead(n):
        return lax.rem(chip + ring(n), chips)

    def behind(n):
        return lax.rem(chip - ring(n) + chips, chips)

    def columns(head):
        return pl.ds(pl.multiple_of(head * HEAD_DIM, HEAD_DIM), HEAD_DIM)

    def peer(other):
        return {"seq": other * 2 + core}

    def segment(offset):
        return {"grp": lax.rem(grp + offset + groups, groups)}

    def slot(block):
        return lax.div(block, 2) + chips * lax.rem(lax.rem(block, 2) + core, 2)

    def remote(src, dst, send, recv, device):
        return pltpu.make_async_remote_copy(
            src_ref=src, dst_ref=dst, send_sem=send, recv_sem=recv, device_id=device, device_id_type=MESH
        )

    def take(ref, sem):
        pltpu.make_async_copy(ref, ref, sem).wait()

    def bring(refs, buf, send, recv, n):
        to = ahead(n)
        for a in range(2):
            remote(refs[a].at[:, columns(to)], buf.at[chip, a], send, recv.at[n], peer(to)).start()

    def give(buf, refs, sems, n):
        to = behind(n)
        for a in range(2):
            remote(buf.at[to, a], refs[a].at[:, columns(chip)], out_send.at[sems], out_recv.at[sems], peer(to)).start()

    def own_in(refs, buf, sem):
        return [pltpu.make_async_copy(refs[a].at[:, columns(chip)], buf.at[chip, a], local.at[sem + a]) for a in range(2)]

    def own_out(buf, refs, sem):
        return [pltpu.make_async_copy(buf.at[chip, a], refs[a].at[:, columns(chip)], local.at[sem + a]) for a in range(2)]

    def show(n):
        return remote(live, bias.at[chip], live_sem.at[0], live_sem.at[1], peer(ahead(n)))

    def swap(buf, sems, s):
        return remote(buf.at[s], buf.at[chips + s], sems.at[0], sems.at[1], mate)

    def anchor_out(a, d):
        dst = key_set.at[a, pl.ds((1 + d) * rows, rows)]
        return remote(anchor_kv.at[a], dst, anchor_sem.at[0], anchor_sem.at[1], segment(d))

    def gterm_out(d):
        return remote(gsend.at[d - 1], grecv.at[d - 1], gterm_sem.at[0], gterm_sem.at[1], segment(-d))

    def gswap():
        return remote(gown, gother, gswap_sem.at[0], gswap_sem.at[1], mate)

    def loop(count, body):
        def step(n, carry):
            body(n)
            return carry

        lax.fori_loop(0, count, step, 0)

    scalars = [
        pltpu.make_async_copy(src, dst, small.at[a])
        for a, (src, dst) in enumerate(((partner_hbm, partner_ref), (anchor_hbm, anchor_ref), (list_hbm, list_ref)))
    ]
    for copy in scalars:
        copy.start()
    inputs_kv, inputs_qg = (k_ref, v_ref), (q_ref, g_ref)
    for copy in own_in(inputs_kv, kv, 0) + own_in(inputs_qg, qg, 2):
        copy.start()

    barrier = pltpu.get_barrier_semaphore()

    def greet(n):
        pl.semaphore_signal(barrier, inc=1, device_id=peer(ahead(n)), device_id_type=MESH)

    pl.semaphore_signal(barrier, inc=1, device_id=mate, device_id_type=MESH)
    loop(others, greet)
    for d in (1, 2, -1, -2):
        pl.semaphore_signal(barrier, inc=1, device_id=segment(d), device_id_type=MESH)
    for copy in scalars:
        copy.wait()
    for d in (1, 2):
        listed = jnp.where((list_ref[0, 0] == d) | (list_ref[0, 1] == d), 0.0, -jnp.inf).astype(F32)
        live[d - 1 : d] = jnp.full((1, HEAD_DIM), listed)
    pl.semaphore_wait(barrier, chips + 4)

    loop(others, lambda n: show(n).start())
    loop(others, lambda n: bring(inputs_kv, kv, in_send.at[0], kv_recv, n))
    loop(others, lambda n: bring(inputs_qg, qg, in_send.at[1], qg_recv, n))
    bias[chip] = live[...]
    gterm[...] = jnp.zeros_like(gterm)

    for copy in own_in(inputs_kv, kv, 0):
        copy.wait()
    swap(kv, swap_sem, chip).start()

    def pass_on(n):
        take(kv.at[behind(n)], kv_recv.at[n])
        swap(kv, swap_sem, behind(n)).start()

    loop(others, pass_on)
    take(kv.at[pl.ds(chips, chips)], swap_sem.at[1])

    anchor = anchor_ref[0]
    anchor_kv[...] = kv[slot(anchor)]
    for d in (1, 2):
        for a in range(2):
            anchor_out(a, d).start()
    for copy in own_in(inputs_qg, qg, 2):
        copy.wait()
    take(bias.at[pl.ds(0, others)], live_sem.at[1])
    take(key_set.at[:, pl.ds(2 * rows, GLOBALS * rows)], anchor_sem.at[1])

    def attend(i):
        n = lax.rem(i + others, chips)
        at = behind(n)

        @pl.when(i > 0)
        def _():
            take(qg.at[at], qg_recv.at[n])

        partner = slot(partner_ref[0, 2 * at + core])
        key_set[:, pl.ds(0, rows)] = kv[at]
        key_set[:, pl.ds(rows, rows)] = kv[partner]
        query, grad, keys, values = qg[at, 0], qg[at, 1], key_set[0], key_set[1]
        scores = matmul(query, keys, 1, 1)
        lane = lax.broadcasted_iota(jnp.int32, (1, HEAD_DIM), 1)
        first, second = bias[at][:1], bias[at][1:]
        offsets = [
            first if at_lane + HEAD_DIM <= rows else second if at_lane >= rows else jnp.where(lane < rows - at_lane, first, second)
            for at_lane in range(0, GLOBALS * rows, HEAD_DIM)
        ]
        offset = jnp.concatenate(offsets, 1)[:, : GLOBALS * rows]
        scores = jnp.concatenate([scores[:, : 2 * rows], scores[:, 2 * rows :] + offset], 1)
        top = jnp.max(scores, axis=1, keepdims=True)
        lifted = jnp.exp2((scores - top) * (scale * LOG2E))
        probs = lifted * (1.0 / jnp.sum(lifted, axis=1, keepdims=True))
        weights = probs.astype(BF16)
        odq[at, 0] = matmul(weights, values, 1, 0).astype(BF16)
        dprob = matmul(grad, values, 1, 1)
        delta = jnp.sum(probs * dprob, axis=1, keepdims=True)
        dscore = (probs * (dprob - delta)).astype(BF16)
        odq[at, 1] = (matmul(dscore, keys, 1, 0) * scale).astype(BF16)
        for a, term in enumerate((matmul(dscore, query, 0, 0) * scale, matmul(weights, grad, 0, 0))):
            own_terms[at, a] = term[:rows]
            terms[at, a] = term[rows : 2 * rows].astype(BF16)
            gterm[a] += term[2 * rows :]

        @pl.when(i > 0)
        def _():
            give(odq, (o_ref, dq_ref), 0, n)

        @pl.when(i == 0)
        def _():
            for copy in own_out(odq, (o_ref, dq_ref), 0):
                copy.start()

        swap(terms, term_sem, at).start()

    loop(chips, attend)

    for d in (1, 2):
        for a in range(2):
            gsend[d - 1, a] = gterm[a, (d - 1) * rows : d * rows].astype(BF16)
        gterm_out(d).start()
    take(grecv, gterm_sem.at[1])
    gown[...] = (grecv[0].astype(F32) + grecv[1].astype(F32)).astype(BF16)
    gswap().start()
    take(terms.at[pl.ds(chips, chips)], term_sem.at[1])
    take(gother, gswap_sem.at[1])

    places = max(chips // 2, 1)
    inner = lax.min(lax.div(lax.rem(lax.div(chip, 2) + 1, places), 2), 1)

    def finish(i):
        n = lax.rem(lax.rem(i + (1 - inner) * (2 * chips - 2 * i), chips) + others, chips)
        at = behind(n)
        block = 2 * at + core
        source = jnp.int32(0)
        for s in range(2 * chips):
            source = jnp.where(partner_ref[0, s] == block, s, source)
        source = slot(source)
        here = jnp.where(anchor == block, 1.0, 0.0).astype(F32)
        back = grecv[0].astype(F32) + grecv[1].astype(F32) + gother[...].astype(F32)
        dkv[at] = (own_terms[at] + terms[source].astype(F32) + here * back).astype(BF16)

        @pl.when(i > 0)
        def _():
            give(dkv, (dk_ref, dv_ref), 1, n)

        @pl.when(i == 0)
        def _():
            for copy in own_out(dkv, (dk_ref, dv_ref), 2):
                copy.start()

    loop(chips, finish)

    for a, buf in enumerate((kv, qg)):
        take(buf.at[pl.ds(0, others)], in_send.at[a])
    take(bias.at[pl.ds(0, others)], live_sem.at[0])
    take(kv.at[pl.ds(0, chips)], swap_sem.at[0])
    take(terms.at[pl.ds(0, chips)], term_sem.at[0])
    take(key_set.at[:, pl.ds(2 * rows, GLOBALS * rows)], anchor_sem.at[0])
    take(gsend, gterm_sem.at[0])
    take(gown, gswap_sem.at[0])
    for copy in own_out(odq, (o_ref, dq_ref), 0) + own_out(dkv, (dk_ref, dv_ref), 2):
        copy.wait()
    for sems in range(2):
        take(odq.at[pl.ds(0, others)], out_send.at[sems])
        take(odq.at[pl.ds(0, others)], out_recv.at[sems])


def write_out(parts, *refs):
    held, arrive, leave = refs[8:]
    height = held.shape[1] // parts

    def each(make):
        return [make(a, pl.ds(p * height, height), a * parts + p) for p in range(parts) for a in range(4)]

    arriving = each(lambda a, at, n: pltpu.make_async_copy(refs[a].at[at], held.at[a, at], arrive.at[n]))
    leaving = each(lambda a, at, n: pltpu.make_async_copy(held.at[a, at], refs[4 + a].at[at], leave.at[n]))
    for copy in arriving:
        copy.start()
    for come, go in zip(arriving, leaving, strict=True):
        come.wait()
        go.start()
    for copy in leaving:
        copy.wait()


def on_device(groups, seats, query_rows, key_rows, value_rows, cotangent, partner, anchors, global_list):
    rows, width = query_rows.shape
    chips = seats // 2
    anywhere = pl.BlockSpec(memory_space=pl.ANY)
    vmem, smem, dma = pltpu.VMEM, pltpu.SMEM, pltpu.SemaphoreType.DMA
    piece = (rows, HEAD_DIM)
    pair = (2, *piece)
    results = pl.pallas_call(
        functools.partial(kernel, groups, chips, rows),
        out_shape=[jax.ShapeDtypeStruct((rows, width), BF16)] * 4,
        in_specs=[anywhere] * 7,
        out_specs=[anywhere] * 4,
        scratch_shapes=[
            smem(partner.shape, jnp.int32),
            smem(anchors.shape, jnp.int32),
            smem(global_list.shape, jnp.int32),
            vmem((2 * chips, *pair), BF16),
            vmem((chips, *pair), BF16),
            vmem((chips, *pair), BF16),
            vmem((chips, *pair), BF16),
            vmem((chips, *pair), F32),
            vmem((2 * chips, *pair), BF16),
            vmem((2, (2 + GLOBALS) * rows, HEAD_DIM), BF16),
            vmem((2, HEAD_DIM), F32),
            vmem((chips, 2, HEAD_DIM), F32),
            vmem(pair, BF16),
            vmem((2, GLOBALS * rows, HEAD_DIM), F32),
            vmem((GLOBALS, *pair), BF16),
            vmem((GLOBALS, *pair), BF16),
            vmem(pair, BF16),
            vmem(pair, BF16),
            dma((3,)),
            dma((4,)),
            dma((2,)),
            dma((chips - 1,)),
            dma((chips - 1,)),
            dma((2,)),
            dma((2,)),
            dma((2,)),
            dma((2,)),
            dma((2,)),
            dma((2,)),
            dma((2,)),
            dma((2,)),
        ],
        compiler_params=pltpu.CompilerParams(collective_id=0, has_side_effects=True, vmem_limit_bytes=VMEM_LIMIT),
        cost_estimate=pl.CostEstimate(flops=3_700_000_000, bytes_accessed=6_300_000, transcendentals=2_400_000),
    )(query_rows, key_rows, value_rows, cotangent, partner, anchors, global_list)
    return pl.pallas_call(
        functools.partial(write_out, PARTS),
        out_shape=[jax.ShapeDtypeStruct((rows, width), BF16)] * 4,
        in_specs=[anywhere] * 4,
        out_specs=[anywhere] * 4,
        scratch_shapes=[vmem((4, rows, width), BF16), dma((4 * PARTS,)), dma((4 * PARTS,))],
    )(*results)


def solution(mesh):
    rows = P(("grp", "seq"), None)
    return jax.shard_map(
        functools.partial(on_device, mesh.shape["grp"], mesh.shape["seq"]),
        mesh=mesh,
        in_specs=(rows, rows, rows, rows, P("grp", None), P("grp"), rows),
        out_specs=(rows, rows, rows, rows),
        check_vma=False,
    )
```

```python
import functools

import jax
import jax.numpy as jnp
from jax import lax
from jax.experimental import pallas as pl
from jax.experimental.pallas import tpu as pltpu
from jax.sharding import PartitionSpec as P

HEAD_DIM = 128
GLOBALS = 2
MESH = pl.DeviceIdType.MESH
LOG2E = 1.4426950408889634
VMEM_LIMIT = 507 * 2**20 // 10
F32, BF16 = jnp.float32, jnp.bfloat16


def matmul(a, b, ca, cb):
    return lax.dot_general(a, b, (((ca,), (cb,)), ((), ())), preferred_element_type=F32)


def kernel(
    groups, chips, rows,
    q_ref, k_ref, v_ref, g_ref, partner_hbm, anchor_hbm, list_hbm,
    o_ref, dq_ref, dk_ref, dv_ref,
    partner_ref, anchor_ref, list_ref,
    kv, qg, odq, dkv, own_terms, terms, key_set, live, bias, anchor_kv, gterm, gsend, grecv, gown, gother,
    small, local, in_send, kv_recv, qg_recv, live_sem, swap_sem, term_sem, anchor_sem, out_send, out_recv,
    gterm_sem, gswap_sem,
):
    seat, grp = lax.axis_index("seq"), lax.axis_index("grp")
    chip, core = lax.div(seat, 2), lax.rem(seat, 2)
    half, others = chips // 2, chips - 1
    scale = HEAD_DIM**-0.5
    mate = {"seq": chip * 2 + (1 - core)}

    def ring(n):
        return half + (2 * lax.rem(n, 2) - 1) * lax.div(n + 1, 2)

    def ahead(n):
        return lax.rem(chip + ring(n), chips)

    def behind(n):
        return lax.rem(chip - ring(n) + chips, chips)

    def columns(head):
        return pl.ds(pl.multiple_of(head * HEAD_DIM, HEAD_DIM), HEAD_DIM)

    def peer(other):
        return {"seq": other * 2 + core}

    def segment(offset):
        return {"grp": lax.rem(grp + offset + groups, groups)}

    def slot(block):
        return lax.div(block, 2) + chips * lax.rem(lax.rem(block, 2) + core, 2)

    def remote(src, dst, send, recv, device):
        return pltpu.make_async_remote_copy(
            src_ref=src, dst_ref=dst, send_sem=send, recv_sem=recv, device_id=device, device_id_type=MESH
        )

    def take(ref, sem):
        pltpu.make_async_copy(ref, ref, sem).wait()

    def bring(refs, buf, send, recv, n):
        to = ahead(n)
        for a in range(2):
            remote(refs[a].at[:, columns(to)], buf.at[chip, a], send, recv.at[n], peer(to)).start()

    def give(buf, refs, sems, n):
        to = behind(n)
        for a in range(2):
            remote(buf.at[to, a], refs[a].at[:, columns(chip)], out_send.at[sems], out_recv.at[sems], peer(to)).start()

    def own_in(refs, buf, sem):
        return [pltpu.make_async_copy(refs[a].at[:, columns(chip)], buf.at[chip, a], local.at[sem + a]) for a in range(2)]

    def own_out(buf, refs, sem):
        return [pltpu.make_async_copy(buf.at[chip, a], refs[a].at[:, columns(chip)], local.at[sem + a]) for a in range(2)]

    def show(n):
        return remote(live, bias.at[chip], live_sem.at[0], live_sem.at[1], peer(ahead(n)))

    def swap(buf, sems, s):
        return remote(buf.at[s], buf.at[chips + s], sems.at[0], sems.at[1], mate)

    def anchor_out(a, d):
        dst = key_set.at[a, pl.ds((1 + d) * rows, rows)]
        return remote(anchor_kv.at[a], dst, anchor_sem.at[0], anchor_sem.at[1], segment(d))

    def gterm_out(d):
        return remote(gsend.at[d - 1], grecv.at[d - 1], gterm_sem.at[0], gterm_sem.at[1], segment(-d))

    def gswap():
        return remote(gown, gother, gswap_sem.at[0], gswap_sem.at[1], mate)

    def loop(count, body):
        def step(n, carry):
            body(n)
            return carry

        lax.fori_loop(0, count, step, 0)

    scalars = [
        pltpu.make_async_copy(src, dst, small.at[a])
        for a, (src, dst) in enumerate(((partner_hbm, partner_ref), (anchor_hbm, anchor_ref), (list_hbm, list_ref)))
    ]
    for copy in scalars:
        copy.start()
    inputs_kv, inputs_qg = (k_ref, v_ref), (q_ref, g_ref)
    for copy in own_in(inputs_kv, kv, 0) + own_in(inputs_qg, qg, 2):
        copy.start()

    barrier = pltpu.get_barrier_semaphore()

    def greet(n):
        pl.semaphore_signal(barrier, inc=1, device_id=peer(ahead(n)), device_id_type=MESH)

    pl.semaphore_signal(barrier, inc=1, device_id=mate, device_id_type=MESH)
    loop(others, greet)
    for d in (1, 2, -1, -2):
        pl.semaphore_signal(barrier, inc=1, device_id=segment(d), device_id_type=MESH)
    for copy in scalars:
        copy.wait()
    for d in (1, 2):
        listed = jnp.where((list_ref[0, 0] == d) | (list_ref[0, 1] == d), 0.0, -jnp.inf).astype(F32)
        live[d - 1 : d] = jnp.full((1, HEAD_DIM), listed)
    pl.semaphore_wait(barrier, chips + 4)

    loop(others, lambda n: show(n).start())
    loop(others, lambda n: bring(inputs_kv, kv, in_send.at[0], kv_recv, n))
    loop(others, lambda n: bring(inputs_qg, qg, in_send.at[1], qg_recv, n))
    bias[chip] = live[...]
    gterm[...] = jnp.zeros_like(gterm)

    for copy in own_in(inputs_kv, kv, 0):
        copy.wait()
    swap(kv, swap_sem, chip).start()

    def pass_on(n):
        take(kv.at[behind(n)], kv_recv.at[n])
        swap(kv, swap_sem, behind(n)).start()

    loop(others, pass_on)
    take(kv.at[pl.ds(chips, chips)], swap_sem.at[1])

    anchor = anchor_ref[0]
    anchor_kv[...] = kv[slot(anchor)]
    for d in (1, 2):
        for a in range(2):
            anchor_out(a, d).start()
    for copy in own_in(inputs_qg, qg, 2):
        copy.wait()
    take(bias.at[pl.ds(0, others)], live_sem.at[1])
    take(key_set.at[:, pl.ds(2 * rows, GLOBALS * rows)], anchor_sem.at[1])

    def attend(i):
        n = lax.rem(i + others, chips)
        at = behind(n)

        @pl.when(i > 0)
        def _():
            take(qg.at[at], qg_recv.at[n])

        partner = slot(partner_ref[0, 2 * at + core])
        key_set[:, pl.ds(0, rows)] = kv[at]
        key_set[:, pl.ds(rows, rows)] = kv[partner]
        query, grad, keys, values = qg[at, 0], qg[at, 1], key_set[0], key_set[1]
        scores = matmul(query, keys, 1, 1)
        lane = lax.broadcasted_iota(jnp.int32, (1, HEAD_DIM), 1)
        first, second = bias[at][:1], bias[at][1:]
        offsets = [
            first if at_lane + HEAD_DIM <= rows else second if at_lane >= rows else jnp.where(lane < rows - at_lane, first, second)
            for at_lane in range(0, GLOBALS * rows, HEAD_DIM)
        ]
        offset = jnp.concatenate(offsets, 1)[:, : GLOBALS * rows]
        scores = jnp.concatenate([scores[:, : 2 * rows], scores[:, 2 * rows :] + offset], 1)
        top = jnp.max(scores, axis=1, keepdims=True)
        lifted = jnp.exp2((scores - top) * (scale * LOG2E))
        probs = lifted * (1.0 / jnp.sum(lifted, axis=1, keepdims=True))
        weights = probs.astype(BF16)
        odq[at, 0] = matmul(weights, values, 1, 0).astype(BF16)
        dprob = matmul(grad, values, 1, 1)
        delta = jnp.sum(probs * dprob, axis=1, keepdims=True)
        dscore = (probs * (dprob - delta)).astype(BF16)
        odq[at, 1] = (matmul(dscore, keys, 1, 0) * scale).astype(BF16)
        for a, term in enumerate((matmul(dscore, query, 0, 0) * scale, matmul(weights, grad, 0, 0))):
            own_terms[at, a] = term[:rows]
            terms[at, a] = term[rows : 2 * rows].astype(BF16)
            gterm[a] += term[2 * rows :]

        @pl.when(i > 0)
        def _():
            give(odq, (o_ref, dq_ref), 0, n)

        @pl.when(i == 0)
        def _():
            for copy in own_out(odq, (o_ref, dq_ref), 0):
                copy.start()

        swap(terms, term_sem, at).start()

    loop(chips, attend)

    for d in (1, 2):
        for a in range(2):
            gsend[d - 1, a] = gterm[a, (d - 1) * rows : d * rows].astype(BF16)
        gterm_out(d).start()
    take(grecv, gterm_sem.at[1])
    gown[...] = (grecv[0].astype(F32) + grecv[1].astype(F32)).astype(BF16)
    gswap().start()
    take(terms.at[pl.ds(chips, chips)], term_sem.at[1])
    take(gother, gswap_sem.at[1])

    places = max(chips // 2, 1)
    inner = lax.min(lax.div(lax.rem(lax.div(chip, 2) + 1, places), 2), 1)

    def finish(i):
        n = lax.rem(lax.rem(i + (1 - inner) * (2 * chips - 2 * i), chips) + others, chips)
        at = behind(n)
        block = 2 * at + core
        source = jnp.int32(0)
        for s in range(2 * chips):
            source = jnp.where(partner_ref[0, s] == block, s, source)
        source = slot(source)
        here = jnp.where(anchor == block, 1.0, 0.0).astype(F32)
        back = grecv[0].astype(F32) + grecv[1].astype(F32) + gother[...].astype(F32)
        dkv[at] = (own_terms[at] + terms[source].astype(F32) + here * back).astype(BF16)

        @pl.when(i > 0)
        def _():
            give(dkv, (dk_ref, dv_ref), 1, n)

        @pl.when(i == 0)
        def _():
            for copy in own_out(dkv, (dk_ref, dv_ref), 2):
                copy.start()

    loop(chips, finish)

    for a, buf in enumerate((kv, qg)):
        take(buf.at[pl.ds(0, others)], in_send.at[a])
    take(bias.at[pl.ds(0, others)], live_sem.at[0])
    take(kv.at[pl.ds(0, chips)], swap_sem.at[0])
    take(terms.at[pl.ds(0, chips)], term_sem.at[0])
    take(key_set.at[:, pl.ds(2 * rows, GLOBALS * rows)], anchor_sem.at[0])
    take(gsend, gterm_sem.at[0])
    take(gown, gswap_sem.at[0])
    for copy in own_out(odq, (o_ref, dq_ref), 0) + own_out(dkv, (dk_ref, dv_ref), 2):
        copy.wait()
    for sems in range(2):
        take(odq.at[pl.ds(0, others)], out_send.at[sems])
        take(odq.at[pl.ds(0, others)], out_recv.at[sems])


def write_out(*refs):
    sems = refs[-1]
    copies = [pltpu.make_async_copy(refs[a], refs[4 + a], sems.at[a]) for a in range(4)]
    for copy in copies:
        copy.start()
    for copy in copies:
        copy.wait()


def on_device(groups, seats, query_rows, key_rows, value_rows, cotangent, partner, anchors, global_list):
    rows, width = query_rows.shape
    chips = seats // 2
    anywhere = pl.BlockSpec(memory_space=pl.ANY)
    vmem, smem, dma = pltpu.VMEM, pltpu.SMEM, pltpu.SemaphoreType.DMA
    piece = (rows, HEAD_DIM)
    pair = (2, *piece)
    results = pl.pallas_call(
        functools.partial(kernel, groups, chips, rows),
        out_shape=[jax.ShapeDtypeStruct((rows, width), BF16)] * 4,
        in_specs=[anywhere] * 7,
        out_specs=[anywhere] * 4,
        scratch_shapes=[
            smem(partner.shape, jnp.int32),
            smem(anchors.shape, jnp.int32),
            smem(global_list.shape, jnp.int32),
            vmem((2 * chips, *pair), BF16),
            vmem((chips, *pair), BF16),
            vmem((chips, *pair), BF16),
            vmem((chips, *pair), BF16),
            vmem((chips, *pair), F32),
            vmem((2 * chips, *pair), BF16),
            vmem((2, (2 + GLOBALS) * rows, HEAD_DIM), BF16),
            vmem((2, HEAD_DIM), F32),
            vmem((chips, 2, HEAD_DIM), F32),
            vmem(pair, BF16),
            vmem((2, GLOBALS * rows, HEAD_DIM), F32),
            vmem((GLOBALS, *pair), BF16),
            vmem((GLOBALS, *pair), BF16),
            vmem(pair, BF16),
            vmem(pair, BF16),
            dma((3,)),
            dma((4,)),
            dma((2,)),
            dma((chips - 1,)),
            dma((chips - 1,)),
            dma((2,)),
            dma((2,)),
            dma((2,)),
            dma((2,)),
            dma((2,)),
            dma((2,)),
            dma((2,)),
            dma((2,)),
        ],
        compiler_params=pltpu.CompilerParams(collective_id=0, has_side_effects=True, vmem_limit_bytes=VMEM_LIMIT),
        cost_estimate=pl.CostEstimate(flops=3_700_000_000, bytes_accessed=6_300_000, transcendentals=2_400_000),
    )(query_rows, key_rows, value_rows, cotangent, partner, anchors, global_list)
    return pl.pallas_call(
        write_out,
        out_shape=[jax.ShapeDtypeStruct((rows, width), BF16)] * 4,
        in_specs=[anywhere] * 4,
        out_specs=[anywhere] * 4,
        scratch_shapes=[dma((4,))],
        compiler_params=pltpu.CompilerParams(vmem_limit_bytes=2**20),
    )(*results)


def solution(mesh):
    rows = P(("grp", "seq"), None)
    return jax.shard_map(
        functools.partial(on_device, mesh.shape["grp"], mesh.shape["seq"]),
        mesh=mesh,
        in_specs=(rows, rows, rows, rows, P("grp", None), P("grp"), rows),
        out_specs=(rows, rows, rows, rows),
        check_vma=False,
    )
```

```python
import functools

import jax
import jax.numpy as jnp
from jax import lax
from jax.experimental import pallas as pl
from jax.experimental.pallas import tpu as pltpu
from jax.sharding import PartitionSpec as P

HEAD_DIM = 128
GLOBALS = 2
MESH = pl.DeviceIdType.MESH
LOG2E = 1.4426950408889634
VMEM_LIMIT = 507 * 2**20 // 10
F32, BF16 = jnp.float32, jnp.bfloat16


def matmul(a, b, ca, cb):
    return lax.dot_general(a, b, (((ca,), (cb,)), ((), ())), preferred_element_type=F32)


def kernel(
    groups, chips, rows,
    q_ref, k_ref, v_ref, g_ref, partner_hbm, anchor_hbm, list_hbm,
    o_ref, dq_ref, dk_ref, dv_ref,
    partner_ref, anchor_ref, list_ref,
    kv, qg, odq, dkv, own_terms, terms, key_set, live, bias, anchor_kv, gterm, gsend, grecv, gown, gother,
    small, local, in_send, kv_recv, qg_recv, live_sem, swap_sem, term_sem, anchor_sem, out_send, out_recv,
    gterm_sem, gswap_sem,
):
    seat, grp = lax.axis_index("seq"), lax.axis_index("grp")
    chip, core = lax.div(seat, 2), lax.rem(seat, 2)
    half, others = chips // 2, chips - 1
    scale = HEAD_DIM**-0.5
    mate = {"seq": chip * 2 + (1 - core)}

    def ring(n):
        return half + (2 * lax.rem(n, 2) - 1) * lax.div(n + 1, 2)

    def ahead(n):
        return lax.rem(chip + ring(n), chips)

    def behind(n):
        return lax.rem(chip - ring(n) + chips, chips)

    def columns(head):
        return pl.ds(pl.multiple_of(head * HEAD_DIM, HEAD_DIM), HEAD_DIM)

    def peer(other):
        return {"seq": other * 2 + core}

    def segment(offset):
        return {"grp": lax.rem(grp + offset + groups, groups)}

    def slot(block):
        return lax.div(block, 2) + chips * lax.rem(lax.rem(block, 2) + core, 2)

    def remote(src, dst, send, recv, device):
        return pltpu.make_async_remote_copy(
            src_ref=src, dst_ref=dst, send_sem=send, recv_sem=recv, device_id=device, device_id_type=MESH
        )

    def take(ref, sem):
        pltpu.make_async_copy(ref, ref, sem).wait()

    def bring(refs, buf, send, recv, n):
        to = ahead(n)
        for a in range(2):
            remote(refs[a].at[:, columns(to)], buf.at[chip, a], send, recv.at[n], peer(to)).start()

    def give(buf, refs, sems, n):
        to = behind(n)
        for a in range(2):
            remote(buf.at[to, a], refs[a].at[:, columns(chip)], out_send.at[sems], out_recv.at[sems], peer(to)).start()

    def own_in(refs, buf, sem):
        return [pltpu.make_async_copy(refs[a].at[:, columns(chip)], buf.at[chip, a], local.at[sem + a]) for a in range(2)]

    def own_out(buf, refs, sem):
        return [pltpu.make_async_copy(buf.at[chip, a], refs[a].at[:, columns(chip)], local.at[sem + a]) for a in range(2)]

    def show(n):
        return remote(live, bias.at[chip], live_sem.at[0], live_sem.at[1], peer(ahead(n)))

    def swap(buf, sems, s):
        return remote(buf.at[s], buf.at[chips + s], sems.at[0], sems.at[1], mate)

    def anchor_out(a, d):
        dst = key_set.at[a, pl.ds((1 + d) * rows, rows)]
        return remote(anchor_kv.at[a], dst, anchor_sem.at[0], anchor_sem.at[1], segment(d))

    def gterm_out(d):
        return remote(gsend.at[d - 1], grecv.at[d - 1], gterm_sem.at[0], gterm_sem.at[1], segment(-d))

    def gswap():
        return remote(gown, gother, gswap_sem.at[0], gswap_sem.at[1], mate)

    def loop(count, body):
        def step(n, carry):
            body(n)
            return carry

        lax.fori_loop(0, count, step, 0)

    barrier = pltpu.get_barrier_semaphore()

    def greet(n):
        pl.semaphore_signal(barrier, inc=1, device_id=peer(ahead(n)), device_id_type=MESH)

    pl.semaphore_signal(barrier, inc=1, device_id=mate, device_id_type=MESH)
    loop(others, greet)
    for d in (1, 2, -1, -2):
        pl.semaphore_signal(barrier, inc=1, device_id=segment(d), device_id_type=MESH)
    scalars = [
        pltpu.make_async_copy(src, dst, small.at[a])
        for a, (src, dst) in enumerate(((partner_hbm, partner_ref), (anchor_hbm, anchor_ref), (list_hbm, list_ref)))
    ]
    for copy in scalars:
        copy.start()
    inputs_kv, inputs_qg = (k_ref, v_ref), (q_ref, g_ref)
    for copy in own_in(inputs_kv, kv, 0) + own_in(inputs_qg, qg, 2):
        copy.start()

    pl.semaphore_wait(barrier, chips + 4)

    loop(others, lambda n: bring(inputs_kv, kv, in_send.at[0], kv_recv, n))
    for copy in scalars:
        copy.wait()
    for d in (1, 2):
        listed = jnp.where((list_ref[0, 0] == d) | (list_ref[0, 1] == d), 0.0, -jnp.inf).astype(F32)
        live[d - 1 : d] = jnp.full((1, HEAD_DIM), listed)
    loop(others, lambda n: show(n).start())
    loop(others, lambda n: bring(inputs_qg, qg, in_send.at[1], qg_recv, n))
    bias[chip] = live[...]
    gterm[...] = jnp.zeros_like(gterm)

    for copy in own_in(inputs_kv, kv, 0):
        copy.wait()
    swap(kv, swap_sem, chip).start()

    def pass_on(n):
        take(kv.at[behind(n)], kv_recv.at[n])
        swap(kv, swap_sem, behind(n)).start()

    loop(others, pass_on)
    take(kv.at[pl.ds(chips, chips)], swap_sem.at[1])

    anchor = anchor_ref[0]
    anchor_kv[...] = kv[slot(anchor)]
    for d in (1, 2):
        for a in range(2):
            anchor_out(a, d).start()
    for copy in own_in(inputs_qg, qg, 2):
        copy.wait()
    take(bias.at[pl.ds(0, others)], live_sem.at[1])
    take(key_set.at[:, pl.ds(2 * rows, GLOBALS * rows)], anchor_sem.at[1])

    def attend(i):
        n = lax.rem(i + others, chips)
        at = behind(n)

        @pl.when(i > 0)
        def _():
            take(qg.at[at], qg_recv.at[n])

        partner = slot(partner_ref[0, 2 * at + core])
        key_set[:, pl.ds(0, rows)] = kv[at]
        key_set[:, pl.ds(rows, rows)] = kv[partner]
        query, grad, keys, values = qg[at, 0], qg[at, 1], key_set[0], key_set[1]
        scores = matmul(query, keys, 1, 1)
        lane = lax.broadcasted_iota(jnp.int32, (1, HEAD_DIM), 1)
        first, second = bias[at][:1], bias[at][1:]
        offsets = [
            first if at_lane + HEAD_DIM <= rows else second if at_lane >= rows else jnp.where(lane < rows - at_lane, first, second)
            for at_lane in range(0, GLOBALS * rows, HEAD_DIM)
        ]
        offset = jnp.concatenate(offsets, 1)[:, : GLOBALS * rows]
        scores = jnp.concatenate([scores[:, : 2 * rows], scores[:, 2 * rows :] + offset], 1)
        top = jnp.max(scores, axis=1, keepdims=True)
        lifted = jnp.exp2((scores - top) * (scale * LOG2E))
        probs = lifted * (1.0 / jnp.sum(lifted, axis=1, keepdims=True))
        weights = probs.astype(BF16)
        odq[at, 0] = matmul(weights, values, 1, 0).astype(BF16)
        dprob = matmul(grad, values, 1, 1)
        delta = jnp.sum(probs * dprob, axis=1, keepdims=True)
        dscore = (probs * (dprob - delta)).astype(BF16)
        odq[at, 1] = (matmul(dscore, keys, 1, 0) * scale).astype(BF16)
        for a, term in enumerate((matmul(dscore, query, 0, 0) * scale, matmul(weights, grad, 0, 0))):
            own_terms[at, a] = term[:rows]
            terms[at, a] = term[rows : 2 * rows].astype(BF16)
            gterm[a] += term[2 * rows :]

        @pl.when(i > 0)
        def _():
            give(odq, (o_ref, dq_ref), 0, n)

        @pl.when(i == 0)
        def _():
            for copy in own_out(odq, (o_ref, dq_ref), 0):
                copy.start()

        swap(terms, term_sem, at).start()

    loop(chips, attend)

    for d in (1, 2):
        for a in range(2):
            gsend[d - 1, a] = gterm[a, (d - 1) * rows : d * rows].astype(BF16)
        gterm_out(d).start()
    take(grecv, gterm_sem.at[1])
    gown[...] = (grecv[0].astype(F32) + grecv[1].astype(F32)).astype(BF16)
    gswap().start()
    take(terms.at[pl.ds(chips, chips)], term_sem.at[1])
    take(gother, gswap_sem.at[1])

    places = max(chips // 2, 1)
    inner = lax.min(lax.div(lax.rem(lax.div(chip, 2) + 1, places), 2), 1)

    def finish(i):
        n = lax.rem(lax.rem(i + (1 - inner) * (2 * chips - 2 * i), chips) + others, chips)
        at = behind(n)
        block = 2 * at + core
        source = jnp.int32(0)
        for s in range(2 * chips):
            source = jnp.where(partner_ref[0, s] == block, s, source)
        source = slot(source)
        here = jnp.where(anchor == block, 1.0, 0.0).astype(F32)
        back = grecv[0].astype(F32) + grecv[1].astype(F32) + gother[...].astype(F32)
        dkv[at] = (own_terms[at] + terms[source].astype(F32) + here * back).astype(BF16)

        @pl.when(i > 0)
        def _():
            give(dkv, (dk_ref, dv_ref), 1, n)

        @pl.when(i == 0)
        def _():
            for copy in own_out(dkv, (dk_ref, dv_ref), 2):
                copy.start()

    loop(chips, finish)

    for a, buf in enumerate((kv, qg)):
        take(buf.at[pl.ds(0, others)], in_send.at[a])
    take(bias.at[pl.ds(0, others)], live_sem.at[0])
    take(kv.at[pl.ds(0, chips)], swap_sem.at[0])
    take(terms.at[pl.ds(0, chips)], term_sem.at[0])
    take(key_set.at[:, pl.ds(2 * rows, GLOBALS * rows)], anchor_sem.at[0])
    take(gsend, gterm_sem.at[0])
    take(gown, gswap_sem.at[0])
    for copy in own_out(odq, (o_ref, dq_ref), 0) + own_out(dkv, (dk_ref, dv_ref), 2):
        copy.wait()
    for sems in range(2):
        take(odq.at[pl.ds(0, others)], out_send.at[sems])
        take(odq.at[pl.ds(0, others)], out_recv.at[sems])


def write_out(*refs):
    sems = refs[-1]
    copies = [pltpu.make_async_copy(refs[a], refs[4 + a], sems.at[a]) for a in range(4)]
    for copy in copies:
        copy.start()
    for copy in copies:
        copy.wait()


def on_device(groups, seats, query_rows, key_rows, value_rows, cotangent, partner, anchors, global_list):
    rows, width = query_rows.shape
    chips = seats // 2
    anywhere = pl.BlockSpec(memory_space=pl.ANY)
    vmem, smem, dma = pltpu.VMEM, pltpu.SMEM, pltpu.SemaphoreType.DMA
    piece = (rows, HEAD_DIM)
    pair = (2, *piece)
    results = pl.pallas_call(
        functools.partial(kernel, groups, chips, rows),
        out_shape=[jax.ShapeDtypeStruct((rows, width), BF16)] * 4,
        in_specs=[anywhere] * 7,
        out_specs=[anywhere] * 4,
        scratch_shapes=[
            smem(partner.shape, jnp.int32),
            smem(anchors.shape, jnp.int32),
            smem(global_list.shape, jnp.int32),
            vmem((2 * chips, *pair), BF16),
            vmem((chips, *pair), BF16),
            vmem((chips, *pair), BF16),
            vmem((chips, *pair), BF16),
            vmem((chips, *pair), F32),
            vmem((2 * chips, *pair), BF16),
            vmem((2, (2 + GLOBALS) * rows, HEAD_DIM), BF16),
            vmem((2, HEAD_DIM), F32),
            vmem((chips, 2, HEAD_DIM), F32),
            vmem(pair, BF16),
            vmem((2, GLOBALS * rows, HEAD_DIM), F32),
            vmem((GLOBALS, *pair), BF16),
            vmem((GLOBALS, *pair), BF16),
            vmem(pair, BF16),
            vmem(pair, BF16),
            dma((3,)),
            dma((4,)),
            dma((2,)),
            dma((chips - 1,)),
            dma((chips - 1,)),
            dma((2,)),
            dma((2,)),
            dma((2,)),
            dma((2,)),
            dma((2,)),
            dma((2,)),
            dma((2,)),
            dma((2,)),
        ],
        compiler_params=pltpu.CompilerParams(collective_id=0, has_side_effects=True, vmem_limit_bytes=VMEM_LIMIT),
        cost_estimate=pl.CostEstimate(flops=3_700_000_000, bytes_accessed=6_300_000, transcendentals=2_400_000),
    )(query_rows, key_rows, value_rows, cotangent, partner, anchors, global_list)
    return pl.pallas_call(
        write_out,
        out_shape=[jax.ShapeDtypeStruct((rows, width), BF16)] * 4,
        in_specs=[anywhere] * 4,
        out_specs=[anywhere] * 4,
        scratch_shapes=[dma((4,))],
        compiler_params=pltpu.CompilerParams(vmem_limit_bytes=2**20),
    )(*results)


def solution(mesh):
    rows = P(("grp", "seq"), None)
    return jax.shard_map(
        functools.partial(on_device, mesh.shape["grp"], mesh.shape["seq"]),
        mesh=mesh,
        in_specs=(rows, rows, rows, rows, P("grp", None), P("grp"), rows),
        out_specs=(rows, rows, rows, rows),
        check_vma=False,
    )
```
